256 devices in a mesh: coarse: 8 (over x, core), sub: 32 (over y, z).
Axes of the slice: x: 4, y: 4, z: 8, core: 2. Of those that a mesh axis runs over, the one named last changes fastest.
Arguments:
- local_operators: bfloat16 [256, 2048, 2048], P(('coarse', 'sub')), as said below
- couplings: bfloat16 [256, 24, 2048], P(('coarse', 'sub')), may hold values from -0.125 to 0.125
- coarse_inverse: float32 [1536, 1536], P('coarse'), as said below
- local_loads: float32 [256, 128, 2048], P(('coarse', 'sub')), may hold values from -6 to 6
- face_lists: int32 [256, 4, 384], P(('coarse', 'sub')), may hold values from 0 to 2047, as said below
- face_counts: int32 [256, 4], P(('coarse', 'sub')), may hold values from 0 to 384, as said below
- corner_map: int32 [256, 24], P(('coarse', 'sub')), may hold values from 0 to 1535
Outputs:
- solution: float32 [256, 128, 2048], P(('coarse', 'sub'))
- residual: float32 [256, 128, 2048], P(('coarse', 'sub'))
The draws below stay inside these ranges and needn't reach their ends.
Inputs may be any that keep to these rules, and one draw needn't show every extreme that they name: `local_operators`: each subdomain's matrix is symmetric and positive definite. `coarse_inverse`: symmetric and positive definite. `face_counts`: the 32 subdomains of one coarse index form a grid of 4 rows of 8; a face's count equals that of the neighbour's matching face and is 0 where the grid has no neighbour on that side; in every draw some face holds exactly 384. `face_lists`: all entries of one subdomain's four lists are distinct; the used slots of a face pair, slot by slot, with the same slots of the neighbour's matching face; slots past the count are to be ignored.
All inputs are finite; a program needn't handle non-finite values.
Results may differ from the reference program's by a relative error of at most 0.025.
Values sent between devices are 32-bit elements; how exact they have to be, the bound alone decides.
A program may use at most 128 MiB of HBM per device.

```python
import jax
import jax.numpy as jnp
from jax import lax

M = 2048
FACE_SLOTS = 384
NCL = 24
LOADS = 128
ITERS = 3
SUBS = 256
GRID_ROW_LENGTH = 8
NCG = 1536
N_COARSE = 8
N_SUB = 32


def symmetric_noise(key, order, spread):
    noise = jax.random.normal(key, (order, order), jnp.float32)
    noise = noise * (spread / order ** 0.5)
    return (noise + noise.T) * 0.70710678


def draw_local_operators(key, part):
    key = jax.random.fold_in(key, 6)

    def single(subkey):
        leading_part, trailing_part = jax.random.split(subkey)
        diagonal = jax.random.uniform(trailing_part, (M,), jnp.float32, 1.5, 4.0)
        return (symmetric_noise(leading_part, M, 0.5) + jnp.diag(diagonal)).astype(jnp.bfloat16)
    return lax.map(single, jax.random.split(key, SUBS))


def draw_coarse_inverse(key, part):
    key = jax.random.fold_in(key, 7)
    leading_part, trailing_part = jax.random.split(key)
    diagonal = jax.random.uniform(trailing_part, (NCG,), jnp.float32, 1.0, 2.0)
    return symmetric_noise(leading_part, NCG, 0.35) + jnp.diag(diagonal)


def draw_face_lists(key, part):
    key = jax.random.fold_in(key, 4)
    shuffled = jax.vmap(lambda subkey: jax.random.permutation(subkey, M))(jax.random.split(key, SUBS))
    return shuffled[:, :4 * FACE_SLOTS].reshape(SUBS, 4, FACE_SLOTS).astype(jnp.int32)


def draw_face_counts(key, part):
    key = jax.random.fold_in(key, 3)
    leading_part, trailing_part = jax.random.split(key)
    horizontal_neighbour = jax.random.randint(leading_part, (N_COARSE, 4, GRID_ROW_LENGTH), FACE_SLOTS // 4, FACE_SLOTS + 1)
    vertical_neighbour = jax.random.randint(trailing_part, (N_COARSE, 4, GRID_ROW_LENGTH), FACE_SLOTS // 4, FACE_SLOTS + 1)
    column_position = lax.broadcasted_iota(jnp.int32, (N_COARSE, 4, GRID_ROW_LENGTH), 2)
    grid_row_index = lax.broadcasted_iota(jnp.int32, (N_COARSE, 4, GRID_ROW_LENGTH), 1)
    horizontal_neighbour = jnp.where(column_position < GRID_ROW_LENGTH - 1, horizontal_neighbour, 0)
    horizontal_neighbour = horizontal_neighbour.at[:, 0, 0].set(FACE_SLOTS)
    vertical_neighbour = jnp.where(grid_row_index < 3, vertical_neighbour, 0)
    empty_column = jnp.zeros((N_COARSE, 4, 1), jnp.int32)
    blank_row_values = jnp.zeros((N_COARSE, 1, GRID_ROW_LENGTH), jnp.int32)
    left_side = jnp.concatenate([empty_column, horizontal_neighbour[:, :, :-1]], axis=2)
    upper_side = jnp.concatenate([blank_row_values, vertical_neighbour[:, :-1, :]], axis=1)
    stacked = jnp.stack([left_side, horizontal_neighbour, upper_side, vertical_neighbour], axis=-1)
    return stacked.reshape(SUBS, 4).astype(jnp.int32)


def place_ends(drawn, rng, low, high):
    index_at = [jax.random.randint(jax.random.fold_in(rng, axis), (), 0, length) for axis, length in enumerate(drawn.shape)]
    main_axis = drawn.shape.index(max(drawn.shape))
    beside = index_at[:main_axis] + [(index_at[main_axis] + 1) % drawn.shape[main_axis]] + index_at[main_axis + 1:]
    return drawn.at[tuple(index_at)].set(low).at[tuple(beside)].set(high)


def block_levels(own_key, dims, cuts, smallest, top_value):
    def one(axis_at, blocks):
        steps = jax.random.uniform(jax.random.fold_in(jax.random.fold_in(own_key, 6), axis_at), (blocks,), jnp.float32, smallest / len(cuts), top_value / len(cuts))
        return jnp.repeat(jnp.exp(steps), dims[axis_at] // blocks).reshape((-1,) + (1,) * (len(dims) - axis_at - 1))

    factor_of = one(*cuts[0])
    for cut in cuts[1:]:
        factor_of = factor_of * one(*cut)
    return factor_of


def centred(own_key, shape, deviation, reach, pieces=(), held_as=jnp.bfloat16):
    level = block_levels(own_key, shape, pieces, -0.22, 0.18) if pieces else 1.0
    values = jax.random.normal(own_key, shape, jnp.float32) * deviation * level
    return jnp.minimum(jnp.maximum(values, -reach), reach).astype(held_as)


def setup_inputs(seed: int = 0) -> dict:
    keys = jax.random.split(jax.random.key(seed), 8)
    return {
        "local_operators": draw_local_operators(jax.random.fold_in(keys[7], 71), 0),
        "couplings": centred(keys[1], (SUBS, NCL, M), M ** -0.5, 0.125, ((0, 256),)),
        "coarse_inverse": draw_coarse_inverse(jax.random.fold_in(keys[7], 71), 0),
        "local_loads": centred(keys[3], (SUBS, LOADS, M), 1.0, 6.0, ((0, 256),), jnp.float32),
        "face_lists": draw_face_lists(jax.random.fold_in(keys[7], 71), 0),
        "face_counts": draw_face_counts(jax.random.fold_in(keys[7], 71), 0),
        "corner_map": place_ends(jax.random.randint(keys[6], (SUBS, NCL), 0, NCG), jax.random.fold_in(keys[6], 1), 0, NCG - 1).astype(jnp.int32),
    }


HIGH = lax.Precision.HIGHEST

def spd_solve(matrix, right):
    factor = jnp.linalg.cholesky(matrix)
    middle = lax.linalg.triangular_solve(factor, right, left_side=True, lower=True)
    return lax.linalg.triangular_solve(factor, middle, left_side=True, lower=True, transpose_a=True)

def spread_faces(values, face_lists, usable):
    height = values.shape[1]
    outgoing = jax.vmap(lambda rows, slots: rows[:, slots])(values, face_lists)
    subdomain_grid = outgoing.reshape((N_COARSE, N_SUB) + outgoing.shape[1:])
    received_values = jnp.stack([jnp.roll(subdomain_grid[:, :, :, 1], 1, axis=1), jnp.roll(subdomain_grid[:, :, :, 0], -1, axis=1), jnp.roll(subdomain_grid[:, :, :, 3], GRID_ROW_LENGTH, axis=1), jnp.roll(subdomain_grid[:, :, :, 2], -GRID_ROW_LENGTH, axis=1)], axis=3)
    received_values = received_values.reshape(outgoing.shape) * usable[:, None]
    return jax.vmap(lambda rows, slots, extra: rows.at[:, slots.reshape(-1)].add(extra.reshape(height, -1)))(values, face_lists, received_values)

def apply_operator(direction, local_operators, couplings, coarse_inverse, corner_map):
    rounded = direction.astype(jnp.bfloat16)
    product = lax.map(lambda pair: jnp.dot(pair[0].astype(jnp.float32), pair[1].astype(jnp.float32), preferred_element_type=jnp.float32), (rounded, local_operators))
    widened = couplings.astype(jnp.float32)
    corner_terms = jnp.einsum('slm,scm->slc', rounded.astype(jnp.float32), widened, precision=HIGH)
    assembled = jnp.zeros((LOADS, NCG), jnp.float32).at[:, corner_map.reshape(-1)].add(jnp.transpose(corner_terms, (1, 0, 2)).reshape(LOADS, -1))
    solved = jnp.dot(assembled, coarse_inverse, precision=HIGH)
    picked = jnp.transpose(solved[:, corner_map], (1, 0, 2))
    image = product + jnp.einsum('slc,scm->slm', picked, widened, precision=HIGH)
    curvature = jnp.einsum('slm,skm->lk', rounded.astype(jnp.float32), image, precision=HIGH)
    return (image, curvature)

def reference(local_operators, couplings, coarse_inverse, local_loads, face_lists, face_counts, corner_map):
    usable = (lax.broadcasted_iota(jnp.int32, face_lists.shape, 2) < face_counts[:, :, None]).astype(jnp.float32)
    shared = jax.vmap(lambda slots, marks: jnp.zeros((M,), jnp.float32).at[slots.reshape(-1)].add(marks.reshape(-1)))(face_lists, usable)
    weight = 1.0 / (1.0 + shared)

    def gram(leading_part, trailing_part):
        return jnp.einsum('slm,skm->lk', leading_part * weight[:, None], trailing_part, precision=HIGH)
    diagonal = jax.vmap(jnp.diagonal)(local_operators).astype(jnp.float32)
    combined = spread_faces(jnp.concatenate([local_loads, diagonal[:, None]], axis=1), face_lists, usable)
    residual = combined[:, :LOADS]
    diagonal_sum = combined[:, LOADS:]
    precond = residual / diagonal_sum
    direction = precond
    precond_gram = gram(precond, residual)
    solution = jnp.zeros_like(residual)
    for iteration in range(ITERS):
        image, curvature = apply_operator(direction, local_operators, couplings, coarse_inverse, corner_map)
        image = spread_faces(image, face_lists, usable)
        step_size = spd_solve(curvature, precond_gram)
        solution = solution + jnp.einsum('lk,slm->skm', step_size, direction, precision=HIGH)
        residual = residual - jnp.einsum('lk,slm->skm', step_size, image, precision=HIGH)
        if iteration + 1 < ITERS:
            precond = residual / diagonal_sum
            fresh = gram(precond, residual)
            blend = spd_solve(precond_gram, fresh)
            direction = precond + jnp.einsum('lk,slm->skm', blend, direction, precision=HIGH)
            precond_gram = fresh
    return (solution, residual)
```

```python
import jax
import jax.numpy as jnp
from jax import lax
from jax.experimental import pallas as pl
from jax.experimental.pallas import tpu as pltpu
from jax.sharding import PartitionSpec as P

ITERS = 3
HIGH = lax.Precision.HIGHEST
MESH = pl.DeviceIdType.MESH
F32, BF16 = jnp.float32, jnp.bfloat16
VMEM = pl.BlockSpec(memory_space=pltpu.VMEM)


def parts_of(values, count):
    parts = []
    for _ in range(count):
        part = lax.reduce_precision(values, 8, 7)
        parts.append(part.astype(BF16))
        values = values - part
    return parts


def greet(groups):
    barrier = pltpu.get_barrier_semaphore()
    for axis, count in groups:
        me = lax.axis_index(axis)

        def one(step, carry, axis=axis, count=count, me=me):
            pl.semaphore_signal(
                barrier,
                inc=1,
                device_id={axis: lax.rem(me + step, count)},
                device_id_type=MESH,
            )
            return carry

        lax.fori_loop(1, count, one, 0)
    pl.semaphore_wait(barrier, sum(count - 1 for _, count in groups))


def send_all(axis, count, pick, landing, sems):
    me = lax.axis_index(axis)

    def one(step, carry):
        peer = lax.rem(me + step, count)
        pltpu.make_async_remote_copy(
            src_ref=pick(peer),
            dst_ref=landing.at[me],
            send_sem=sems.at[0],
            recv_sem=sems.at[1],
            device_id={axis: peer},
            device_id_type=MESH,
        ).start()
        return carry

    lax.fori_loop(1, count, one, 0)


def wait_all(count, landing, sems):
    whole = landing.at[pl.ds(0, count - 1)]
    pltpu.make_async_copy(whole, whole, sems.at[1]).wait()
    pltpu.make_async_copy(whole, whole, sems.at[0]).wait()


def sum_slots(count, landing):
    total = landing[0]
    for slot in range(1, count):
        total = total + landing[slot]
    return total


def stacked_dot(rows, matrix):
    first = rows.astype(BF16).astype(F32)
    rest = rows - first
    second = rest.astype(BF16).astype(F32)
    third = rest - second
    stack = jnp.concatenate([first, second, third, jnp.zeros_like(rows)], axis=0).astype(BF16)
    full = jnp.dot(stack, matrix, preferred_element_type=F32)
    return full[0:4] + full[4:8] + full[8:12]


def all_sum_kernel(n_sub, n_coarse, x_ref, out_ref, first, middle, second, sems):
    me, group = lax.axis_index("sub"), lax.axis_index("coarse")
    greet((("sub", n_sub), ("coarse", n_coarse)))
    first[me] = x_ref[me]
    send_all("sub", n_sub, lambda peer: x_ref.at[peer], first, sems.at[0])
    wait_all(n_sub, first, sems.at[0])
    partial = sum_slots(n_sub, first)
    middle[...] = partial
    second[group] = partial
    send_all("coarse", n_coarse, lambda peer: middle, second, sems.at[1])
    wait_all(n_coarse, second, sems.at[1])
    total = sum_slots(n_coarse, second)
    middle[...] = total
    out_ref[me] = total
    send_all("sub", n_sub, lambda peer: middle, out_ref, sems.at[2])
    wait_all(n_sub, out_ref, sems.at[2])


def all_sum(x, sizes, collective_id):
    n_sub, n_coarse = sizes
    height, width = x.shape
    rows = height // n_sub
    slots = lambda count: pltpu.VMEM((count, rows, width), F32)
    out = pl.pallas_call(
        lambda *refs: all_sum_kernel(n_sub, n_coarse, *refs),
        out_shape=jax.ShapeDtypeStruct((n_sub, rows, width), F32),
        in_specs=[VMEM],
        out_specs=VMEM,
        scratch_shapes=[
            slots(n_sub),
            pltpu.VMEM((rows, width), F32),
            slots(n_coarse),
            pltpu.SemaphoreType.DMA((3, 2)),
        ],
        compiler_params=pltpu.CompilerParams(collective_id=collective_id, has_side_effects=True),
    )(x.reshape(n_sub, rows, width))
    return out.reshape(height, width)


def gather_kernel(n_sub, x_ref, out_ref, sems):
    me = lax.axis_index("sub")
    greet((("sub", n_sub),))
    out_ref[me] = x_ref[...]
    send_all("sub", n_sub, lambda peer: x_ref, out_ref, sems)
    wait_all(n_sub, out_ref, sems)


def gather_group(x, n_sub, collective_id):
    return pl.pallas_call(
        lambda *refs: gather_kernel(n_sub, *refs),
        out_shape=jax.ShapeDtypeStruct((n_sub,) + x.shape, x.dtype),
        in_specs=[VMEM],
        out_specs=VMEM,
        scratch_shapes=[pltpu.SemaphoreType.DMA((2,))],
        compiler_params=pltpu.CompilerParams(collective_id=collective_id, has_side_effects=True),
    )(x)


def corner_kernel(
    n_sub, n_coarse, terms_ref, spread_ref, pick_ref, inverse_ref, out_ref,
    first, partial_rows, second, solved_rows, third, picks, sems,
):
    me, group = lax.axis_index("sub"), lax.axis_index("coarse")
    greet((("sub", n_sub), ("coarse", n_coarse)))
    first[me] = terms_ref[me]
    send_all("sub", n_sub, lambda peer: terms_ref.at[peer], first, sems.at[0])
    wait_all(n_sub, first, sems.at[0])
    tiles = [
        first[4 * t] + first[4 * t + 1] + first[4 * t + 2] + first[4 * t + 3]
        for t in range(n_sub // 4)
    ]
    partial = stacked_dot(jnp.concatenate(tiles, axis=1), spread_ref[...])
    partial_rows[...] = partial
    second[group] = partial
    send_all("coarse", n_coarse, lambda peer: partial_rows, second, sems.at[1])
    wait_all(n_coarse, second, sems.at[1])
    assembled = sum_slots(n_coarse, second)
    wide = stacked_dot(assembled, inverse_ref[...])
    solved = wide[:, 0:256] + wide[:, 256:512] + wide[:, 512:768]
    solved_rows[...] = solved
    third[group] = solved
    send_all("coarse", n_coarse, lambda peer: solved_rows, third, sems.at[2])
    wait_all(n_coarse, third, sems.at[2])
    everything = jnp.concatenate([third[c] for c in range(n_coarse)], axis=1)
    picked = stacked_dot(everything, pick_ref[...])
    for t in range(n_sub // 4):
        picks[t] = picked[:, 128 * t : 128 * (t + 1)]
    out_ref[me] = picks[me // 4]
    send_all("sub", n_sub, lambda peer: picks.at[peer // 4], out_ref, sems.at[3])
    wait_all(n_sub, out_ref, sems.at[3])


def corner_solve(terms, spread, pick, inverse, sizes, collective_id):
    n_sub, n_coarse = sizes
    height, width = terms.shape
    rows = height // n_sub
    span = spread.shape[1]
    out = pl.pallas_call(
        lambda *refs: corner_kernel(n_sub, n_coarse, *refs),
        out_shape=jax.ShapeDtypeStruct((n_sub, rows, width), F32),
        in_specs=[VMEM] * 4,
        out_specs=VMEM,
        scratch_shapes=[
            pltpu.VMEM((n_sub, rows, width), F32),
            pltpu.VMEM((rows, span), F32),
            pltpu.VMEM((n_coarse, rows, span), F32),
            pltpu.VMEM((rows, 256), F32),
            pltpu.VMEM((n_coarse, rows, 256), F32),
            pltpu.VMEM((n_sub // 4, rows, width), F32),
            pltpu.SemaphoreType.DMA((4, 2)),
        ],
        compiler_params=pltpu.CompilerParams(
            collective_id=collective_id, has_side_effects=True, vmem_limit_bytes=40 << 20
        ),
    )(terms.reshape(n_sub, rows, width), spread, pick, inverse)
    return out.reshape(height, width)


def solve_kernel(matrix_ref, right_ref, out_ref, work):
    size = matrix_ref.shape[0]
    work[:, 0:size] = matrix_ref[...]
    work[:, size : 2 * size] = right_ref[...]
    row_at = lax.broadcasted_iota(jnp.int32, (size, 1), 0)

    def block(step, carry):
        left = work[:, 0:size]
        right = work[:, size : 2 * size]
        for inner in range(8):
            pivot_at = step * 8 + inner
            mark = row_at == pivot_at
            start = pl.multiple_of(step * 8, 8)
            column = left[:, inner : inner + 1]
            pivot_left = jnp.sum(jnp.where(mark, left, 0.0), axis=0, keepdims=True)
            pivot_right = jnp.sum(jnp.where(mark, right, 0.0), axis=0, keepdims=True)
            scale = 1.0 / pivot_left[:, inner : inner + 1]
            pivot_left = pivot_left * scale
            pivot_right = pivot_right * scale
            left = jnp.where(mark, pivot_left, left - column * pivot_left)
            right = jnp.where(mark, pivot_right, right - column * pivot_right)
        work[:, 0:size] = pltpu.roll(left, size - 8, 1)
        work[:, size : 2 * size] = right
        return carry

    lax.fori_loop(0, size // 8, block, 0)
    out_ref[...] = work[:, size : 2 * size]


def spd_solve(matrix, right):
    size = matrix.shape[0]
    return pl.pallas_call(
        solve_kernel,
        out_shape=jax.ShapeDtypeStruct(right.shape, F32),
        in_specs=[VMEM, VMEM],
        out_specs=VMEM,
        scratch_shapes=[pltpu.VMEM((size, 2 * size), F32)],
    )(matrix, right)


def shifted(value, axis, steps):
    count = lax.axis_size(axis)
    first, last = (max(0, -steps), min(count, count - steps))
    return lax.ppermute(value, axis, [(source, source + steps) for source in range(first, last)])


def local(
    local_operators, couplings, coarse_inverse, local_loads, face_lists, face_counts, corner_map
):
    operator_block = local_operators[0]
    coupling = couplings[0]
    slot_lists = face_lists[0]
    face_total, slot_total = slot_lists.shape
    width = operator_block.shape[0]
    loads = local_loads.shape[1]
    corners = coupling.shape[0]
    n_sub, n_coarse = lax.axis_size("sub"), lax.axis_size("coarse")
    sizes = (n_sub, n_coarse)
    row_length = n_sub // 4
    me = lax.axis_index("sub")

    usable = lax.broadcasted_iota(jnp.int32, (face_total, slot_total), 1) < face_counts[0][:, None]
    marked = jnp.where(usable, slot_lists, -1).reshape(-1)
    hot = (
        marked[:, None] == lax.broadcasted_iota(jnp.int32, (face_total * slot_total, width), 1)
    ).astype(BF16)
    weight = 1.0 / (1.0 + jnp.sum(hot.astype(F32), axis=0))[None]

    rows = coarse_inverse.shape[0]
    maps = jnp.full((1, 128), -1, jnp.int32).at[:, :corners].set(corner_map)
    every = gather_group(maps, n_sub, 0)[:, 0, :32].reshape(-1)
    place = jnp.where(every < 0, -1, every // rows * 256 + every % rows)
    span = n_coarse * 256
    spread = (place[:, None] == lax.broadcasted_iota(jnp.int32, (n_sub * 32, span), 1)).astype(BF16)
    pick = (place[None, :] == lax.broadcasted_iota(jnp.int32, (span, n_sub * 32), 0)).astype(BF16)
    turned = coarse_inverse.T.reshape(n_coarse, rows, rows)
    turned = jnp.pad(turned, ((0, 0), (0, 256 - rows), (0, 256 - rows))).reshape(span, 256)
    inverse = jnp.concatenate(parts_of(turned, 3), axis=1)
    coupling_at = lax.dynamic_update_slice(
        jnp.zeros((128, width), BF16), coupling, (lax.rem(me, 4) * 32, 0)
    )

    def assemble(values, count):
        height = values.shape[0]
        pieces = jnp.concatenate(parts_of(values, count), axis=0)
        outgoing = lax.dot_general(
            pieces, hot, (((1,), (1,)), ((), ())), preferred_element_type=F32
        )
        outgoing = outgoing.reshape(count, height, -1).sum(0)
        outgoing = outgoing.reshape(height, face_total, slot_total)
        received = jnp.concatenate(
            [
                shifted(outgoing[:, 1], "sub", 1),
                shifted(outgoing[:, 0], "sub", -1),
                shifted(outgoing[:, 3], "sub", row_length),
                shifted(outgoing[:, 2], "sub", -row_length),
            ],
            axis=1,
        )
        pieces = jnp.concatenate(parts_of(received, count), axis=0)
        added = jnp.dot(pieces, hot, preferred_element_type=F32)
        return values + added.reshape(count, height, -1).sum(0)

    def cross(leading, trailing):
        return jnp.einsum("lm,km->lk", leading, trailing, precision=HIGH)

    block = 128
    diagonal = jnp.concatenate(
        [
            jnp.sum(
                jnp.where(
                    jnp.eye(block, dtype=bool),
                    operator_block[at : at + block, at : at + block].astype(F32),
                    0.0,
                ),
                axis=0,
            )
            for at in range(0, width, block)
        ]
    )[None]
    combined = assemble(jnp.concatenate([local_loads[0], diagonal], axis=0), 3)
    residual = combined[:loads]
    scaled = weight / combined[loads:]
    inverse_diagonal = 1.0 / combined[loads:]
    precond = residual * inverse_diagonal
    direction = precond
    precond_gram = all_sum(cross(residual * scaled, residual), sizes, 1)
    solution = jnp.zeros_like(residual)
    for iteration in range(ITERS):
        last = iteration + 1 == ITERS
        rounded = direction.astype(BF16)
        terms = lax.dot_general(
            rounded, coupling_at, (((1,), (1,)), ((), ())), preferred_element_type=F32
        )
        picked = corner_solve(terms, spread, pick, inverse, sizes, 2)
        product = jnp.dot(rounded, operator_block, preferred_element_type=F32)
        image = product + jnp.dot(picked, coupling_at.astype(F32), precision=HIGH)
        curvature = cross(rounded.astype(F32), image)
        image = assemble(image, 2)
        if last:
            curvature = all_sum(curvature, sizes, 1)
        else:
            weighted = image * scaled
            sums = jnp.concatenate(
                [curvature, cross(weighted, residual), cross(weighted, image)], axis=1
            )
            sums = all_sum(sums, sizes, 3)
            curvature, mixed, square = sums[:, :loads], sums[:, loads : 2 * loads], sums[:, 2 * loads :]
        step_size = spd_solve(curvature, precond_gram)
        solution = solution + jnp.einsum("lk,lm->km", step_size, direction, precision=HIGH)
        residual = residual - jnp.einsum("lk,lm->km", step_size, image, precision=HIGH)
        if not last:
            turn = jnp.dot(step_size.T, mixed, precision=HIGH)
            fresh = (
                precond_gram
                - turn
                - turn.T
                + jnp.dot(step_size.T, jnp.dot(square, step_size, precision=HIGH), precision=HIGH)
            )
            blend = spd_solve(precond_gram, fresh)
            direction = residual * inverse_diagonal + jnp.einsum(
                "lk,lm->km", blend, direction, precision=HIGH
            )
            precond_gram = fresh
    return (solution[None], residual[None])


def solution(mesh):
    return jax.shard_map(
        local,
        mesh=mesh,
        in_specs=(
            P(("coarse", "sub"), None, None),
            P(("coarse", "sub"), None, None),
            P("coarse", None),
            P(("coarse", "sub"), None, None),
            P(("coarse", "sub"), None, None),
            P(("coarse", "sub"), None),
            P(("coarse", "sub"), None),
        ),
        out_specs=(P(("coarse", "sub"), None, None), P(("coarse", "sub"), None, None)),
        check_vma=False,
    )
```

```python
import jax
import jax.numpy as jnp
from jax import lax
from jax.experimental import pallas as pl
from jax.experimental.pallas import tpu as pltpu
from jax.sharding import PartitionSpec as P

ITERS = 3
HIGH = lax.Precision.HIGHEST
MESH = pl.DeviceIdType.MESH
F32, BF16, I32 = jnp.float32, jnp.bfloat16, jnp.int32
VMEM = pl.BlockSpec(memory_space=pltpu.VMEM)
TILE = 256
LANES = 128


def high_and_rest(values):
    first = values.astype(BF16).astype(F32)
    return first, values - first


def nt(left, right, precision=None):
    return lax.dot_general(
        left, right, (((1,), (1,)), ((), ())), preferred_element_type=F32, precision=precision
    )


def nn(left, right, precision=None):
    return jnp.dot(left, right, preferred_element_type=F32, precision=precision)


def lanes(step, size):
    return pl.ds(pl.multiple_of(step * size, size), size)


def loop(count, body):
    def one(step, carry):
        body(step)
        return carry

    lax.fori_loop(0, count, one, 0)


def greet(groups):
    barrier = pltpu.get_barrier_semaphore()
    for axis, count in groups:
        me = lax.axis_index(axis)

        def one(step, carry, axis=axis, count=count, me=me):
            pl.semaphore_signal(
                barrier,
                inc=1,
                device_id={axis: lax.rem(me + step, count)},
                device_id_type=MESH,
            )
            return carry

        lax.fori_loop(1, count, one, 0)
    pl.semaphore_wait(barrier, sum(count - 1 for _, count in groups))


def send_all(axis, count, pick, landing, sems):
    me = lax.axis_index(axis)

    def one(step, carry):
        peer = lax.rem(me + step, count)
        pltpu.make_async_remote_copy(
            src_ref=pick(peer),
            dst_ref=landing.at[me],
            send_sem=sems.at[0],
            recv_sem=sems.at[1],
            device_id={axis: peer},
            device_id_type=MESH,
        ).start()
        return carry

    lax.fori_loop(1, count, one, 0)


def wait_all(count, landing, sems):
    whole = landing.at[pl.ds(0, count - 1)]
    pltpu.make_async_copy(whole, whole, sems.at[1]).wait()
    pltpu.make_async_copy(whole, whole, sems.at[0]).wait()


def sum_slots(count, landing):
    total = landing[0]
    for slot in range(1, count):
        total = total + landing[slot]
    return total


def stacked_dot(rows, matrix, dot):
    first, rest = high_and_rest(rows)
    second, third = high_and_rest(rest)
    stack = jnp.concatenate([first, second, third, jnp.zeros_like(rows)], axis=0).astype(BF16)
    full = dot(stack, matrix)
    return full[0:4] + full[4:8] + full[8:12]


def eliminate(work, first, last):
    size = work.shape[0]
    row_at = lax.broadcasted_iota(I32, (8, 1), 0)

    def block(step, carry):
        at = pl.ds(pl.multiple_of(step * 8, 8), 8)
        panel = work[at, :]
        for k in range(8):
            row = panel[k : k + 1, :]
            row = row * (1.0 / row[:, k : k + 1])
            panel = jnp.where(row_at == k, row, panel - panel[:, k : k + 1] * row)
        full = work[...]
        left, right = full[:, 0:size], full[:, size:]
        for k in range(8):
            column = full[:, k : k + 1]
            left = left - column * panel[k : k + 1, 0:size]
            right = right - column * panel[k : k + 1, size:]
        work[:, 0:size] = pltpu.roll(left, size - 8, 1)
        work[:, size:] = right
        work[at, 0:size] = pltpu.roll(panel[:, 0:size], size - 8, 1)
        work[at, size:] = panel[:, size:]
        return carry

    lax.fori_loop(first, last, block, 0)


def body(
    n_sub, n_coarse,
    operator, coupling, coarse_rows, loads, lists, maps,
    solution, residual,
    hot, spread, pick, inverse, near, direction, rounded, product, image, pieces,
    face_out, face_in, invd, scaled, gram, blend, picked, terms_mine,
    terms, terms_in, part_rows, part_in, solved_rows, solved_in, picks, picks_in,
    sums, sums_in, mid_rows, mid_in, sums_out, maps_in, solver, inverter, sems, face_sems,
):
    me, group = lax.axis_index("sub"), lax.axis_index("coarse")
    height, width = loads.shape
    corners = coupling.shape[0]
    slots = hot.shape[1]
    span = slots // 4
    row_length = n_sub // 4
    tiles = n_sub // 4
    column, row = lax.rem(me, row_length), me // row_length
    sides = (
        (-1, column > 0),
        (1, column < row_length - 1),
        (-row_length, row > 0),
        (row_length, row < 3),
    )

    def faces_start(rows):
        for face, (shift, there) in enumerate(sides):
            other = face ^ 1

            @pl.when(there)
            def _(face=face, shift=shift, other=other):
                pltpu.make_async_remote_copy(
                    src_ref=face_out.at[pl.ds(0, rows), pl.ds(face * span, span)],
                    dst_ref=face_in.at[pl.ds(0, rows), pl.ds(other * span, span)],
                    send_sem=face_sems.at[0, face],
                    recv_sem=face_sems.at[1, other],
                    device_id={"sub": me + shift},
                    device_id_type=MESH,
                ).start()

    def faces_wait(rows):
        for face, (_, there) in enumerate(sides):

            @pl.when(there)
            def _(face=face):
                view = face_in.at[pl.ds(0, rows), pl.ds(face * span, span)]
                pltpu.make_async_copy(view, view, face_sems.at[1, face]).wait()
                pltpu.make_async_copy(view, view, face_sems.at[0, face]).wait()

    def gather(rows):
        def one(step):
            at = lanes(step, TILE)
            full = nn(pieces[0 : 2 * rows, :], hot[:, at])
            face_out[0:rows, at] = full[0:rows] + full[rows : 2 * rows]

        loop(slots // TILE, one)

    def scatter_rows(rows, store):
        first, rest = high_and_rest(face_in[0:rows, :])
        pieces[0:rows, 0:slots] = first.astype(BF16)
        pieces[rows : 2 * rows, 0:slots] = rest.astype(BF16)

        def one(step):
            at = lanes(step, TILE)
            full = nt(pieces[0 : 2 * rows, 0:slots], hot[at, :])
            store(at, full[0:rows] + full[rows : 2 * rows])

        loop(width // TILE, one)

    def all_sum_start():
        sums_in[me] = sums[me]
        send_all("sub", n_sub, lambda peer: sums.at[peer], sums_in, sems.at[4])

    def all_sum_finish():
        wait_all(n_sub, sums_in, sems.at[4])
        partial = sum_slots(n_sub, sums_in)
        mid_rows[...] = partial
        mid_in[group] = partial
        send_all("coarse", n_coarse, lambda peer: mid_rows, mid_in, sems.at[5])
        wait_all(n_coarse, mid_in, sems.at[5])
        total = sum_slots(n_coarse, mid_in)
        mid_rows[...] = total
        sums_out[me] = total
        send_all("sub", n_sub, lambda peer: mid_rows, sums_out, sems.at[6])
        wait_all(n_sub, sums_out, sems.at[6])

    face_in[...] = jnp.zeros_like(face_in)
    greet((("sub", n_sub), ("coarse", n_coarse)))
    maps_in[me] = maps[...]
    send_all("sub", n_sub, lambda peer: maps, maps_in, sems.at[7])

    def build_hot(step):
        at = lanes(step, LANES)
        index = lax.broadcasted_iota(I32, (width, LANES), 0)
        hot[:, at] = jnp.where(index == lists[:, at], 1.0, 0.0).astype(BF16)

    loop(slots // LANES, build_hot)
    eye = lax.broadcasted_iota(I32, (LANES, LANES), 0) == lax.broadcasted_iota(
        I32, (LANES, LANES), 1
    )
    face_rows = height + 8 + corners
    image[...] = jnp.zeros_like(image)
    for at in range(0, width, LANES):
        block = operator[at : at + LANES, at : at + LANES].astype(F32)
        image[0:1, at : at + LANES] = jnp.sum(jnp.where(eye, block, 0.0), axis=0, keepdims=True)
    values = jnp.concatenate([loads[...], image[0:8, :], coupling[...]], axis=0)
    first, rest = high_and_rest(values)
    pieces[0:face_rows, :] = first.astype(BF16)
    pieces[face_rows : 2 * face_rows, :] = rest.astype(BF16)
    gather(face_rows)
    faces_start(face_rows)
    rows_of = coarse_rows.shape[0]
    first, rest = high_and_rest(coarse_rows[...])
    inverse[...] = jnp.zeros_like(inverse)
    inverse[0:rows_of, :] = first.astype(BF16)
    inverse[256 : 256 + rows_of, :] = rest.astype(BF16)
    wait_all(n_sub, maps_in, sems.at[7])
    for t in range(tiles):
        both = sum_slots(4, maps_in.at[pl.ds(4 * t, 4)])
        at = slice(LANES * t, LANES * (t + 1))
        index = lax.broadcasted_iota(I32, (spread.shape[0], LANES), 0) + 1
        spread[:, at] = jnp.where(index == both[0:1, :], 1.0, 0.0).astype(BF16)
        index = lax.broadcasted_iota(I32, (pick.shape[0], LANES), 0) + 1
        pick[:, at] = jnp.where(index == both[1:2, :], 1.0, 0.0).astype(BF16)
    faces_wait(face_rows)

    product[...] = jnp.zeros_like(product)
    for face in range(4):
        at = slice(face * span, (face + 1) * span)
        product[corners * (face + 1) : corners * (face + 2), at] = face_in[height + 8 : face_rows, at]
    rounded[...] = product[...].astype(BF16)

    def build_near(step):
        at = lanes(step, TILE)
        tile = nt(rounded[:, 0:slots], hot[at, :])
        both = jnp.concatenate([coupling[:, at], tile[corners:]], axis=0)
        near[:, at] = both.astype(BF16)

    loop(width // TILE, build_near)

    rows = height + 16

    def finish_setup(at, added):
        combined = loads[:, at] + added[0:height]
        diagonal = image[0:1, at] + added[height : height + 1]
        residual[:, at] = combined
        invd[:, at] = 1.0 / diagonal
        direction[:, at] = combined / diagonal
        rounded[:, at] = direction[:, at].astype(BF16)
        solution[:, at] = jnp.zeros_like(combined)

    ones = jnp.ones((16, slots), BF16)

    def build_weight(step):
        at = lanes(step, TILE)
        scaled[:, at] = 1.0 / (1.0 + nt(ones, hot[at, :])[0:1])

    loop(width // TILE, build_weight)
    scatter_rows(rows, finish_setup)
    scaled[...] = scaled[...] * invd[...]
    start = nt(residual[...] * scaled[...], residual[...], HIGH)
    sums[...] = jnp.zeros_like(sums)
    for p in range(n_sub):
        sums[p, :, 0:LANES] = start[4 * p : 4 * p + 4, :]
    all_sum_start()
    all_sum_finish()
    for p in range(n_sub):
        gram[4 * p : 4 * p + 4, :] = sums_out[p, :, 0:LANES]

    lane_at = lax.broadcasted_iota(I32, (8, LANES), 1)
    own_lanes = lax.broadcasted_iota(I32, (height, LANES), 1) < corners
    slot_of = lax.rem(me, 4)

    def iteration(turn):
        mine = jnp.where(own_lanes, nt(rounded[...], near[...]), 0.0)
        terms_mine[...] = mine
        placed = mine
        for q in range(1, 4):
            placed = jnp.where(slot_of == q, pltpu.roll(mine, 32 * q, 1), placed)
        for p in range(n_sub):
            terms[p] = placed[4 * p : 4 * p + 4, :]
        terms_in[me] = terms[me]
        send_all("sub", n_sub, lambda peer: terms.at[peer], terms_in, sems.at[0])

        def multiply(step):
            at = lanes(step, TILE)
            tile = nn(rounded[...], operator[:, at])
            product[:, at] = tile
            first, rest = high_and_rest(tile)
            pieces[0:height, at] = first.astype(BF16)
            pieces[height : 2 * height, at] = rest.astype(BF16)

        loop(width // TILE, multiply)
        wait_all(n_sub, terms_in, sems.at[0])
        row_tiles = [sum_slots(4, terms_in.at[pl.ds(4 * t, 4)]) for t in range(tiles)]
        partial = stacked_dot(jnp.concatenate(row_tiles, axis=1), spread[...], nt)
        part_rows[...] = partial
        part_in[group] = partial
        send_all("coarse", n_coarse, lambda peer: part_rows, part_in, sems.at[1])
        gather(height)
        faces_start(height)
        wait_all(n_coarse, part_in, sems.at[1])
        wide = stacked_dot(sum_slots(n_coarse, part_in), inverse[...], nt)
        solved = wide[:, 0:256] + wide[:, 256:512]
        solved_rows[...] = solved
        solved_in[group] = solved
        send_all("coarse", n_coarse, lambda peer: solved_rows, solved_in, sems.at[2])
        both = nt(rounded[...], pieces[0 : 2 * height, :])
        curvature = both[:, 0:height] + both[:, height : 2 * height]
        inverter[:, 0:height] = gram[...]
        inverter[:, height:] = jnp.where(eye, 1.0, 0.0)
        eliminate(inverter, 0, 4)
        wait_all(n_coarse, solved_in, sems.at[2])
        everything = jnp.concatenate([solved_in[c] for c in range(n_coarse)], axis=1)
        chosen = stacked_dot(everything, pick[...], nn)
        doubled = jnp.concatenate([chosen, chosen], axis=0)
        for peer in range(n_sub):
            at_row, at_column = divmod(peer, row_length)
            sources = [(peer, 0)]
            if at_column > 0:
                sources.append((peer - 1, 1))
            if at_column < row_length - 1:
                sources.append((peer + 1, 2))
            if at_row > 0:
                sources.append((peer - row_length, 3))
            if at_row < 3:
                sources.append((peer + row_length, 4))
            total = jnp.zeros((8, LANES), F32)
            for source, place in sources:
                t = source // 4
                tile = doubled[:, LANES * t : LANES * (t + 1)]
                shift = (corners * place - 32 * (source % 4)) % LANES
                if shift:
                    tile = pltpu.roll(tile, shift, 1)
                here = (lane_at >= corners * place) & (lane_at < corners * (place + 1))
                total = jnp.where(here, tile, total)
            picks[peer] = total[0:4]
        picks_in[me] = picks[me]
        send_all("sub", n_sub, lambda peer: picks.at[peer], picks_in, sems.at[3])
        faces_wait(height)

        def add_faces(at, added):
            image[:, at] = product[:, at] + added

        scatter_rows(height, add_faces)
        eliminate(inverter, 4, 8)
        wait_all(n_sub, picks_in, sems.at[3])
        for p in range(n_sub):
            picked[4 * p : 4 * p + 4, :] = picks_in[p]
        curvature = curvature + nt(
            terms_mine[...], jnp.where(own_lanes, picked[...], 0.0), HIGH
        )
        first, rest = high_and_rest(picked[...])
        stack = jnp.concatenate([first, rest], axis=0).astype(BF16)

        def add_corners(step):
            at = lanes(step, TILE)
            full = nn(stack, near[:, at])
            image[:, at] = image[:, at] + full[0:height] + full[height : 2 * height]

        loop(width // TILE, add_corners)
        weighted = image[...] * scaled[...]
        mixed = nt(weighted, residual[...], HIGH)
        square = nt(weighted, image[...], HIGH)
        for p in range(n_sub):
            part = slice(4 * p, 4 * p + 4)
            sums[p, :, 0:LANES] = curvature[part, :]
            sums[p, :, LANES : 2 * LANES] = mixed[part, :]
            sums[p, :, 2 * LANES : 3 * LANES] = square[part, :]
        all_sum_start()
        eliminate(inverter, 8, 16)
        all_sum_finish()
        for p in range(n_sub):
            part = slice(4 * p, 4 * p + 4)
            solver[part, 0:LANES] = sums_out[p, :, 0:LANES]
        solver[:, height:] = gram[...]
        eliminate(solver, 0, height // 8)
        step_size = solver[:, height:]
        step_turned = step_size.T

        @pl.when(turn < ITERS - 1)
        def _():
            for p in range(n_sub):
                part = slice(4 * p, 4 * p + 4)
                solver[part, :] = sums_out[p, :, LANES : 3 * LANES]
            cross = nn(step_turned, solver[:, 0:LANES], HIGH)
            twice = nn(step_turned, nn(solver[:, LANES:], step_size, HIGH), HIGH)
            fresh = gram[...] - cross - cross.T + twice
            blend[...] = nn(fresh, inverter[:, height:], HIGH)
            gram[...] = fresh

        factors = jnp.concatenate([step_turned, blend[...]], axis=0)

        def update(step):
            at = lanes(step, TILE)
            moved = nn(factors, direction[:, at], HIGH)
            solution[:, at] = solution[:, at] + moved[0:height]
            left = residual[:, at] - nn(step_turned, image[:, at], HIGH)
            residual[:, at] = left
            ahead = left * invd[:, at] + moved[height : 2 * height]
            direction[:, at] = ahead
            rounded[:, at] = ahead.astype(BF16)

        loop(width // TILE, update)

    blend[...] = jnp.zeros_like(blend)
    loop(ITERS, iteration)


def local(
    local_operators, couplings, coarse_inverse, local_loads, face_lists, face_counts, corner_map
):
    slot_lists = face_lists[0]
    face_total, slot_total = slot_lists.shape
    _, height, width = local_loads.shape
    corners = couplings.shape[1]
    n_sub, n_coarse = lax.axis_size("sub"), lax.axis_size("coarse")
    slots = face_total * slot_total
    rows, coarse_total = coarse_inverse.shape
    face_rows = height + 8 + corners
    split = n_sub // 4 * LANES

    usable = lax.broadcasted_iota(I32, (face_total, slot_total), 1) < face_counts[0][:, None]
    marked = jnp.where(usable, slot_lists, -1).reshape(1, slots)
    place = corner_map // rows * 256 + corner_map % rows
    both = jnp.concatenate([corner_map, place], axis=0) + 1
    maps = lax.dynamic_update_slice(
        jnp.zeros((2, LANES), I32), both, (0, lax.rem(lax.axis_index("sub"), 4) * 32)
    )
    result = [jax.ShapeDtypeStruct((height, width), F32)] * 2
    per = height // n_sub
    scratch = [
        pltpu.VMEM((width, slots), BF16),
        pltpu.VMEM((coarse_total, split), BF16),
        pltpu.VMEM((n_coarse * 256, split), BF16),
        pltpu.VMEM((512, coarse_total), BF16),
        pltpu.VMEM((LANES, width), BF16),
        pltpu.VMEM((height, width), F32),
        pltpu.VMEM((height, width), BF16),
        pltpu.VMEM((height, width), F32),
        pltpu.VMEM((height, width), F32),
        pltpu.VMEM((2 * face_rows, width), BF16),
        pltpu.VMEM((face_rows, slots), F32),
        pltpu.VMEM((face_rows, slots), F32),
        pltpu.VMEM((1, width), F32),
        pltpu.VMEM((1, width), F32),
        pltpu.VMEM((height, height), F32),
        pltpu.VMEM((height, height), F32),
        pltpu.VMEM((height, LANES), F32),
        pltpu.VMEM((height, LANES), F32),
        pltpu.VMEM((n_sub, per, LANES), F32),
        pltpu.VMEM((n_sub, per, LANES), F32),
        pltpu.VMEM((per, coarse_total), F32),
        pltpu.VMEM((n_coarse, per, coarse_total), F32),
        pltpu.VMEM((per, 256), F32),
        pltpu.VMEM((n_coarse, per, 256), F32),
        pltpu.VMEM((n_sub, per, LANES), F32),
        pltpu.VMEM((n_sub, per, LANES), F32),
        pltpu.VMEM((n_sub, per, 3 * height), F32),
        pltpu.VMEM((n_sub, per, 3 * height), F32),
        pltpu.VMEM((per, 3 * height), F32),
        pltpu.VMEM((n_coarse, per, 3 * height), F32),
        pltpu.VMEM((n_sub, per, 3 * height), F32),
        pltpu.VMEM((n_sub, 2, LANES), I32),
        pltpu.VMEM((height, 2 * height), F32),
        pltpu.VMEM((height, 2 * height), F32),
        pltpu.SemaphoreType.DMA((8, 2)),
        pltpu.SemaphoreType.DMA((2, 4)),
    ]
    solved, left = pl.pallas_call(
        lambda *refs: body(n_sub, n_coarse, *refs),
        out_shape=result,
        in_specs=[VMEM] * 6,
        out_specs=[VMEM] * 2,
        scratch_shapes=scratch,
        compiler_params=pltpu.CompilerParams(
            collective_id=0, has_side_effects=True, vmem_limit_bytes=60 << 20
        ),
    )(local_operators[0], couplings[0].astype(F32), coarse_inverse, local_loads[0], marked, maps)
    return (solved[None], left[None])


def solution(mesh):
    return jax.shard_map(
        local,
        mesh=mesh,
        in_specs=(
            P(("coarse", "sub"), None, None),
            P(("coarse", "sub"), None, None),
            P("coarse", None),
            P(("coarse", "sub"), None, None),
            P(("coarse", "sub"), None, None),
            P(("coarse", "sub"), None),
            P(("coarse", "sub"), None),
        ),
        out_specs=(P(("coarse", "sub"), None, None), P(("coarse", "sub"), None, None)),
        check_vma=False,
    )
```

```python
import jax
import jax.numpy as jnp
from jax import lax
from jax.experimental import pallas as pl
from jax.experimental.pallas import tpu as pltpu
from jax.sharding import PartitionSpec as P

ITERS = 3
HIGHEST = lax.Precision.HIGHEST
HIGH = lax.Precision.HIGH
MESH = pl.DeviceIdType.MESH
F32, BF16, I32 = jnp.float32, jnp.bfloat16, jnp.int32
VMEM = pl.BlockSpec(memory_space=pltpu.VMEM)
TILE = 256
LANES = 128


def high_and_rest(values):
    first = values.astype(BF16).astype(F32)
    return first, values - first


def nt(left, right, precision=None):
    return lax.dot_general(
        left, right, (((1,), (1,)), ((), ())), preferred_element_type=F32, precision=precision
    )


def nn(left, right, precision=None):
    return jnp.dot(left, right, preferred_element_type=F32, precision=precision)


def lanes(step, size):
    return pl.ds(pl.multiple_of(step * size, size), size)


def loop(count, body):
    def one(step, carry):
        body(step)
        return carry

    lax.fori_loop(0, count, one, 0)


def greet(groups):
    barrier = pltpu.get_barrier_semaphore()
    for axis, count in groups:
        me = lax.axis_index(axis)

        def one(step, carry, axis=axis, count=count, me=me):
            pl.semaphore_signal(
                barrier,
                inc=1,
                device_id={axis: lax.rem(me + step, count)},
                device_id_type=MESH,
            )
            return carry

        lax.fori_loop(1, count, one, 0)


def await_greetings(groups):
    pl.semaphore_wait(pltpu.get_barrier_semaphore(), sum(count - 1 for _, count in groups))


def send_all(axis, count, pick, landing, sems):
    me = lax.axis_index(axis)

    def one(step, carry):
        peer = lax.rem(me + step, count)
        pltpu.make_async_remote_copy(
            src_ref=pick(peer),
            dst_ref=landing.at[me],
            send_sem=sems.at[0],
            recv_sem=sems.at[1],
            device_id={axis: peer},
            device_id_type=MESH,
        ).start()
        return carry

    lax.fori_loop(1, count, one, 0)


def wait_all(count, landing, sems):
    whole = landing.at[pl.ds(0, count - 1)]
    pltpu.make_async_copy(whole, whole, sems.at[1]).wait()
    pltpu.make_async_copy(whole, whole, sems.at[0]).wait()


def sum_slots(count, landing, wide=None):
    total = landing[0, :, 0:wide]
    for slot in range(1, count):
        total = total + landing[slot, :, 0:wide]
    return total


def stacked_dot(rows, matrix, dot):
    first, rest = high_and_rest(rows)
    second, third = high_and_rest(rest)
    stack = jnp.concatenate([first, second, third, jnp.zeros_like(rows)], axis=0).astype(BF16)
    full = dot(stack, matrix)
    return full[0:4] + full[4:8] + full[8:12]


def eliminate(work, first, last):
    size = work.shape[0]
    steps = size // 8
    row_at = lax.broadcasted_iota(I32, (8, 1), 0)

    def rows(step):
        return pl.ds(pl.multiple_of(step * 8, 8), 8)

    def reduce(panel):
        columns = [jnp.broadcast_to(panel[:, j : j + 1], (8, size)) for j in range(8)]
        left, right = panel[:, 0:size], panel[:, size:]
        for k in range(8):
            column = columns[k]
            inverse = 1.0 / column[k : k + 1, :]

            def clear(values, k=k, column=column, inverse=inverse):
                row = values[k : k + 1, :] * inverse
                return jnp.where(row_at == k, row, values - column * row)

            for j in range(k + 1, 8):
                columns[j] = clear(columns[j])
            left, right = clear(left), clear(right)
        return jnp.concatenate([left, right], axis=1)

    def less(values, panel):
        out = values
        for k in range(8):
            out = out - values[:, k : k + 1] * panel[k : k + 1, :]
        return out

    def rolled(values):
        return jnp.concatenate([pltpu.roll(values[:, 0:size], size - 8, 1), values[:, size:]], axis=1)

    def block(step, panel):
        following = rows(jnp.minimum(step + 1, steps - 1))
        upcoming = reduce(rolled(less(work[following, :], panel)))
        work[...] = rolled(less(work[...], panel))
        work[rows(step), :] = rolled(panel)
        return upcoming

    lax.fori_loop(first, last, block, reduce(work[rows(first), :]))


def body(
    n_sub, n_coarse,
    operator_there, coupling, coarse_rows, loads, lists, maps,
    solution, residual,
    operator, hot, spread, pick, inverse, near, direction, rounded, product, image, pieces,
    face_out, face_in, invd, scaled, gram, blend, picked, terms_mine,
    terms, terms_in, part_rows, part_in, solved_rows, solved_in, picks, picks_in,
    sums, sums_in, mid_rows, rows_in, mid_in, sums_out, maps_in, solver, inverter, sems, face_sems, load_sem,
):
    me, group = lax.axis_index("sub"), lax.axis_index("coarse")
    height, width = loads.shape
    corners = coupling.shape[0]
    slots = hot.shape[1]
    span = slots // 4
    row_length = n_sub // 4
    tiles = n_sub // 4
    column, row = lax.rem(me, row_length), me // row_length
    sides = (
        (-1, column > 0),
        (1, column < row_length - 1),
        (-row_length, row > 0),
        (row_length, row < 3),
    )

    def faces_start(rows):
        for face, (shift, there) in enumerate(sides):
            other = face ^ 1

            @pl.when(there)
            def _(face=face, shift=shift, other=other):
                pltpu.make_async_remote_copy(
                    src_ref=face_out.at[pl.ds(0, rows), pl.ds(face * span, span)],
                    dst_ref=face_in.at[pl.ds(0, rows), pl.ds(other * span, span)],
                    send_sem=face_sems.at[0, face],
                    recv_sem=face_sems.at[1, other],
                    device_id={"sub": me + shift},
                    device_id_type=MESH,
                ).start()

    def faces_wait(rows):
        for face, (_, there) in enumerate(sides):

            @pl.when(there)
            def _(face=face):
                view = face_in.at[pl.ds(0, rows), pl.ds(face * span, span)]
                pltpu.make_async_copy(view, view, face_sems.at[1, face]).wait()
                pltpu.make_async_copy(view, view, face_sems.at[0, face]).wait()

    def gather(rows):
        def one(step):
            at = lanes(step, TILE)
            full = nn(pieces[0 : 2 * rows, :], hot[:, at])
            face_out[0:rows, at] = full[0:rows] + full[rows : 2 * rows]

        loop(slots // TILE, one)

    def scatter_rows(rows, store):
        first, rest = high_and_rest(face_in[0:rows, :])
        pieces[0:rows, 0:slots] = first.astype(BF16)
        pieces[rows : 2 * rows, 0:slots] = rest.astype(BF16)

        def one(step):
            at = lanes(step, TILE)
            full = nt(pieces[0 : 2 * rows, 0:slots], hot[at, :])
            store(at, full[0:rows] + full[rows : 2 * rows])

        loop(width // TILE, one)

    per = height // row_length

    def part_of(index):
        return pl.ds(pl.multiple_of(index * per, per), per)

    def sum_parts(count, landing, wide):
        total = landing[0:per, 0:wide]
        for slot in range(1, count):
            total = total + landing[slot * per : (slot + 1) * per, 0:wide]
        return total

    def send_group(count, own, device, source, landing, sem, wide):
        def one(step, carry):
            peer = lax.rem(own + step, count)
            pltpu.make_async_remote_copy(
                src_ref=source(peer),
                dst_ref=landing.at[part_of(own), pl.ds(0, wide)],
                send_sem=sem.at[0],
                recv_sem=sem.at[1],
                device_id=device(peer),
                device_id_type=MESH,
            ).start()
            return carry

        lax.fori_loop(1, count, one, 0)

    def wait_group(count, landing, sem, wide):
        whole = landing.at[pl.ds(0, (count - 1) * per), pl.ds(0, wide)]
        pltpu.make_async_copy(whole, whole, sem.at[1]).wait()
        pltpu.make_async_copy(whole, whole, sem.at[0]).wait()

    def in_row(peer):
        return {"sub": row * row_length + peer}

    def in_column(peer):
        return {"sub": peer * row_length + column}

    def in_groups(peer):
        return {"coarse": peer}

    def all_sum_start(wide):
        sums_in[part_of(column), 0:wide] = sums[part_of(column), 0:wide]
        source = lambda peer: sums.at[part_of(peer), pl.ds(0, wide)]
        send_group(row_length, column, in_row, source, sums_in, sems.at[4], wide)

    def all_sum_finish(wide):
        wait_group(row_length, sums_in, sems.at[4], wide)
        total = sum_parts(row_length, sums_in, wide)
        stages = (
            (4, row, in_column, rows_in, sems.at[8]),
            (n_coarse, group, in_groups, mid_in, sems.at[5]),
        )
        for stage, (count, own, device, landing, sem) in enumerate(stages):
            mid_rows[stage, :, 0:wide] = total
            landing[part_of(own), 0:wide] = total
            source = lambda peer, stage=stage: mid_rows.at[stage, :, pl.ds(0, wide)]
            send_group(count, own, device, source, landing, sem, wide)
            wait_group(count, landing, sem, wide)
            total = sum_parts(count, landing, wide)
        mid_rows[2, :, 0:wide] = total
        sums_out[part_of(column), 0:wide] = total
        source = lambda peer: mid_rows.at[2, :, pl.ds(0, wide)]
        send_group(row_length, column, in_row, source, sums_out, sems.at[6], wide)
        wait_group(row_length, sums_out, sems.at[6], wide)

    face_in[...] = jnp.zeros_like(face_in)
    greet((("sub", n_sub), ("coarse", n_coarse)))
    load = pltpu.make_async_copy(operator_there, operator, load_sem)
    load.start()
    maps_in[me] = maps[...]

    def build_hot(step):
        at = lanes(step, LANES)
        index = lax.broadcasted_iota(I32, (width, LANES), 0)
        hot[:, at] = jnp.where(index == lists[:, at], 1.0, 0.0).astype(BF16)

    loop(slots // LANES, build_hot)
    eye = lax.broadcasted_iota(I32, (LANES, LANES), 0) == lax.broadcasted_iota(
        I32, (LANES, LANES), 1
    )
    face_rows = height + 8 + corners
    image[...] = jnp.zeros_like(image)
    rows_of = coarse_rows.shape[0]
    first, rest = high_and_rest(coarse_rows[...])
    inverse[...] = jnp.zeros_like(inverse)
    inverse[0:rows_of, :] = first.astype(BF16)
    inverse[256 : 256 + rows_of, :] = rest.astype(BF16)
    load.wait()
    for at in range(0, width, LANES):
        block = operator[at : at + LANES, at : at + LANES].astype(F32)
        image[0:1, at : at + LANES] = jnp.sum(jnp.where(eye, block, 0.0), axis=0, keepdims=True)
    values = jnp.concatenate([loads[...], image[0:8, :], coupling[...]], axis=0)
    first, rest = high_and_rest(values)
    pieces[0:face_rows, :] = first.astype(BF16)
    pieces[face_rows : 2 * face_rows, :] = rest.astype(BF16)
    gather(face_rows)
    await_greetings((("sub", n_sub), ("coarse", n_coarse)))
    faces_start(face_rows)
    send_all("sub", n_sub, lambda peer: maps, maps_in, sems.at[7])
    wait_all(n_sub, maps_in, sems.at[7])
    for t in range(tiles):
        both = sum_slots(4, maps_in.at[pl.ds(4 * t, 4)])
        at = slice(LANES * t, LANES * (t + 1))
        index = lax.broadcasted_iota(I32, (spread.shape[0], LANES), 0) + 1
        spread[:, at] = jnp.where(index == both[0:1, :], 1.0, 0.0).astype(BF16)
        index = lax.broadcasted_iota(I32, (pick.shape[0], LANES), 0) + 1
        pick[:, at] = jnp.where(index == both[1:2, :], 1.0, 0.0).astype(BF16)
    faces_wait(face_rows)

    product[...] = jnp.zeros_like(product)
    for face in range(4):
        at = slice(face * span, (face + 1) * span)
        product[corners * (face + 1) : corners * (face + 2), at] = face_in[height + 8 : face_rows, at]
    rounded[...] = product[...].astype(BF16)

    def build_near(step):
        at = lanes(step, TILE)
        tile = nt(rounded[:, 0:slots], hot[at, :])
        both = jnp.concatenate([coupling[:, at], tile[corners:]], axis=0)
        near[:, at] = both.astype(BF16)

    loop(width // TILE, build_near)

    rows = height + 16

    def finish_setup(at, added):
        combined = loads[:, at] + added[0:height]
        diagonal = image[0:1, at] + added[height : height + 1]
        residual[:, at] = combined
        invd[:, at] = 1.0 / diagonal
        direction[:, at] = combined / diagonal
        rounded[:, at] = direction[:, at].astype(BF16)
        solution[:, at] = jnp.zeros_like(combined)

    ones = jnp.ones((16, slots), BF16)

    def build_weight(step):
        at = lanes(step, TILE)
        scaled[:, at] = 1.0 / (1.0 + nt(ones, hot[at, :])[0:1])

    loop(width // TILE, build_weight)
    scatter_rows(rows, finish_setup)
    scaled[...] = scaled[...] * invd[...]
    start = nt(residual[...] * scaled[...], residual[...], HIGHEST)
    for p in range(n_sub):
        part = slice(4 * p, 4 * p + 4)
        sums[part, 0:LANES] = start[part, :]
    all_sum_start(LANES)
    all_sum_finish(LANES)
    gram[...] = sums_out[:, 0:LANES]

    lane_at = lax.broadcasted_iota(I32, (8, LANES), 1)
    own_lanes = lax.broadcasted_iota(I32, (height, LANES), 1) < corners
    slot_of = lax.rem(me, 4)

    def iteration(turn):
        mine = jnp.where(own_lanes, nt(rounded[...], near[...]), 0.0)
        terms_mine[...] = mine
        placed = mine
        for q in range(1, 4):
            placed = jnp.where(slot_of == q, pltpu.roll(mine, 32 * q, 1), placed)
        for p in range(n_sub):
            terms[p] = placed[4 * p : 4 * p + 4, :]
        terms_in[me] = terms[me]
        send_all("sub", n_sub, lambda peer: terms.at[peer], terms_in, sems.at[0])

        def multiply(step):
            at = lanes(step, TILE)
            tile = nn(rounded[...], operator[:, at])
            product[:, at] = tile
            first, rest = high_and_rest(tile)
            pieces[0:height, at] = first.astype(BF16)
            pieces[height : 2 * height, at] = rest.astype(BF16)

        loop(width // TILE, multiply)
        wait_all(n_sub, terms_in, sems.at[0])
        row_tiles = [sum_slots(4, terms_in.at[pl.ds(4 * t, 4)]) for t in range(tiles)]
        partial = stacked_dot(jnp.concatenate(row_tiles, axis=1), spread[...], nt)
        part_rows[...] = partial
        part_in[group] = partial
        send_all("coarse", n_coarse, lambda peer: part_rows, part_in, sems.at[1])
        gather(height)
        faces_start(height)
        wait_all(n_coarse, part_in, sems.at[1])
        wide = stacked_dot(sum_slots(n_coarse, part_in), inverse[...], nt)
        solved = wide[:, 0:256] + wide[:, 256:512]
        solved_rows[...] = solved
        solved_in[group] = solved
        send_all("coarse", n_coarse, lambda peer: solved_rows, solved_in, sems.at[2])
        both = nt(rounded[...], pieces[0 : 2 * height, :])
        curvature = both[:, 0:height] + both[:, height : 2 * height]
        inverter[:, 0:height] = gram[...]
        inverter[:, height:] = jnp.where(eye, 1.0, 0.0)
        eliminate(inverter, 0, 4)
        wait_all(n_coarse, solved_in, sems.at[2])
        everything = jnp.concatenate([solved_in[c] for c in range(n_coarse)], axis=1)
        chosen = stacked_dot(everything, pick[...], nn)
        doubled = jnp.concatenate([chosen, chosen], axis=0)
        for peer in range(n_sub):
            at_row, at_column = divmod(peer, row_length)
            sources = [(peer, 0)]
            if at_column > 0:
                sources.append((peer - 1, 1))
            if at_column < row_length - 1:
                sources.append((peer + 1, 2))
            if at_row > 0:
                sources.append((peer - row_length, 3))
            if at_row < 3:
                sources.append((peer + row_length, 4))
            total = jnp.zeros((8, LANES), F32)
            for source, place in sources:
                t = source // 4
                tile = doubled[:, LANES * t : LANES * (t + 1)]
                shift = (corners * place - 32 * (source % 4)) % LANES
                if shift:
                    tile = pltpu.roll(tile, shift, 1)
                here = (lane_at >= corners * place) & (lane_at < corners * (place + 1))
                total = jnp.where(here, tile, total)
            picks[peer] = total[0:4]
        picks_in[me] = picks[me]
        send_all("sub", n_sub, lambda peer: picks.at[peer], picks_in, sems.at[3])
        faces_wait(height)

        def add_faces(at, added):
            image[:, at] = product[:, at] + added

        scatter_rows(height, add_faces)
        eliminate(inverter, 4, 8)
        wait_all(n_sub, picks_in, sems.at[3])
        for p in range(n_sub):
            picked[4 * p : 4 * p + 4, :] = picks_in[p]
        curvature = curvature + nt(
            terms_mine[...], jnp.where(own_lanes, picked[...], 0.0), HIGH
        )
        first, rest = high_and_rest(picked[...])
        stack = jnp.concatenate([first, rest], axis=0).astype(BF16)

        def add_corners(step):
            at = lanes(step, TILE)
            full = nn(stack, near[:, at])
            image[:, at] = image[:, at] + full[0:height] + full[height : 2 * height]

        loop(width // TILE, add_corners)
        for p in range(n_sub):
            part = slice(4 * p, 4 * p + 4)
            sums[part, 0:LANES] = curvature[part, :]

        @pl.when(turn < ITERS - 1)
        def _():
            weighted = image[...] * scaled[...]
            mixed = nt(weighted, residual[...], HIGH)
            square = nt(weighted, image[...], HIGH)
            for p in range(n_sub):
                part = slice(4 * p, 4 * p + 4)
                sums[part, LANES : 2 * LANES] = mixed[part, :]
                sums[part, 2 * LANES :] = square[part, :]
            all_sum_start(3 * LANES)
            eliminate(inverter, 8, 16)
            all_sum_finish(3 * LANES)

        @pl.when(turn == ITERS - 1)
        def _():
            all_sum_start(LANES)
            all_sum_finish(LANES)

        solver[:, 0:LANES] = sums_out[:, 0:LANES]
        solver[:, height:] = gram[...]
        eliminate(solver, 0, height // 8)
        step_size = solver[:, height:]
        step_turned = step_size.T

        @pl.when(turn < ITERS - 1)
        def _():
            cross = nn(step_turned, sums_out[:, LANES : 2 * LANES], HIGHEST)
            twice = nn(step_turned, nn(sums_out[:, 2 * LANES :], step_size, HIGHEST), HIGHEST)
            fresh = gram[...] - cross - cross.T + twice
            blend[...] = nn(fresh, inverter[:, height:], HIGHEST)
            gram[...] = fresh

        factors = jnp.concatenate([step_turned, blend[...]], axis=0)

        def update(step):
            at = lanes(step, TILE)
            moved = nn(factors, direction[:, at], HIGH)
            solution[:, at] = solution[:, at] + moved[0:height]
            left = residual[:, at] - nn(step_turned, image[:, at], HIGH)
            residual[:, at] = left
            ahead = left * invd[:, at] + moved[height : 2 * height]
            direction[:, at] = ahead
            rounded[:, at] = ahead.astype(BF16)

        loop(width // TILE, update)

    blend[...] = jnp.zeros_like(blend)
    loop(ITERS, iteration)


def local(
    local_operators, couplings, coarse_inverse, local_loads, face_lists, face_counts, corner_map
):
    slot_lists = face_lists[0]
    face_total, slot_total = slot_lists.shape
    _, height, width = local_loads.shape
    corners = couplings.shape[1]
    n_sub, n_coarse = lax.axis_size("sub"), lax.axis_size("coarse")
    slots = face_total * slot_total
    rows, coarse_total = coarse_inverse.shape
    face_rows = height + 8 + corners
    split = n_sub // 4 * LANES

    usable = lax.broadcasted_iota(I32, (face_total, slot_total), 1) < face_counts[0][:, None]
    marked = jnp.where(usable, slot_lists, -1).reshape(1, slots)
    place = corner_map // rows * 256 + corner_map % rows
    both = jnp.concatenate([corner_map, place], axis=0) + 1
    maps = lax.dynamic_update_slice(
        jnp.zeros((2, LANES), I32), both, (0, lax.rem(lax.axis_index("sub"), 4) * 32)
    )
    result = [jax.ShapeDtypeStruct((height, width), F32)] * 2
    per = height // n_sub
    scratch = [
        pltpu.VMEM((width, width), BF16),
        pltpu.VMEM((width, slots), BF16),
        pltpu.VMEM((coarse_total, split), BF16),
        pltpu.VMEM((n_coarse * 256, split), BF16),
        pltpu.VMEM((512, coarse_total), BF16),
        pltpu.VMEM((LANES, width), BF16),
        pltpu.VMEM((height, width), F32),
        pltpu.VMEM((height, width), BF16),
        pltpu.VMEM((height, width), F32),
        pltpu.VMEM((height, width), F32),
        pltpu.VMEM((2 * face_rows, width), BF16),
        pltpu.VMEM((face_rows, slots), F32),
        pltpu.VMEM((face_rows, slots), F32),
        pltpu.VMEM((1, width), F32),
        pltpu.VMEM((1, width), F32),
        pltpu.VMEM((height, height), F32),
        pltpu.VMEM((height, height), F32),
        pltpu.VMEM((height, LANES), F32),
        pltpu.VMEM((height, LANES), F32),
        pltpu.VMEM((n_sub, per, LANES), F32),
        pltpu.VMEM((n_sub, per, LANES), F32),
        pltpu.VMEM((per, coarse_total), F32),
        pltpu.VMEM((n_coarse, per, coarse_total), F32),
        pltpu.VMEM((per, 256), F32),
        pltpu.VMEM((n_coarse, per, 256), F32),
        pltpu.VMEM((n_sub, per, LANES), F32),
        pltpu.VMEM((n_sub, per, LANES), F32),
        pltpu.VMEM((8 * (height // 8), 3 * height), F32),
        pltpu.VMEM((8 * (height // 8), 3 * height), F32),
        pltpu.VMEM((3, height // 8, 3 * height), F32),
        pltpu.VMEM((4 * (height // 8), 3 * height), F32),
        pltpu.VMEM((n_coarse * (height // 8), 3 * height), F32),
        pltpu.VMEM((8 * (height // 8), 3 * height), F32),
        pltpu.VMEM((n_sub, 2, LANES), I32),
        pltpu.VMEM((height, 2 * height), F32),
        pltpu.VMEM((height, 2 * height), F32),
        pltpu.SemaphoreType.DMA((9, 2)),
        pltpu.SemaphoreType.DMA((2, 4)),
        pltpu.SemaphoreType.DMA,
    ]
    solved, left = pl.pallas_call(
        lambda *refs: body(n_sub, n_coarse, *refs),
        out_shape=result,
        in_specs=[pl.BlockSpec(memory_space=pl.ANY)] + [VMEM] * 5,
        out_specs=[VMEM] * 2,
        scratch_shapes=scratch,
        compiler_params=pltpu.CompilerParams(
            collective_id=0, has_side_effects=True, vmem_limit_bytes=60 << 20
        ),
    )(local_operators[0], couplings[0].astype(F32), coarse_inverse, local_loads[0], marked, maps)
    return (solved[None], left[None])


def solution(mesh):
    return jax.shard_map(
        local,
        mesh=mesh,
        in_specs=(
            P(("coarse", "sub"), None, None),
            P(("coarse", "sub"), None, None),
            P("coarse", None),
            P(("coarse", "sub"), None, None),
            P(("coarse", "sub"), None, None),
            P(("coarse", "sub"), None),
            P(("coarse", "sub"), None),
        ),
        out_specs=(P(("coarse", "sub"), None, None), P(("coarse", "sub"), None, None)),
        check_vma=False,
    )
```

```python
import jax
import jax.numpy as jnp
from jax import lax
from jax.experimental import pallas as pl
from jax.experimental.pallas import tpu as pltpu
from jax.sharding import PartitionSpec as P

ITERS = 3
HIGHEST = lax.Precision.HIGHEST
HIGH = lax.Precision.HIGH
MESH = pl.DeviceIdType.MESH
F32, BF16, I32 = jnp.float32, jnp.bfloat16, jnp.int32
VMEM = pl.BlockSpec(memory_space=pltpu.VMEM)
TILE = 256
LANES = 128


def high_and_rest(values):
    first = values.astype(BF16).astype(F32)
    return first, values - first


def nt(left, right, precision=None):
    return lax.dot_general(
        left, right, (((1,), (1,)), ((), ())), preferred_element_type=F32, precision=precision
    )


def nn(left, right, precision=None):
    return jnp.dot(left, right, preferred_element_type=F32, precision=precision)


def lanes(step, size):
    return pl.ds(pl.multiple_of(step * size, size), size)


def loop(count, body):
    def one(step, carry):
        body(step)
        return carry

    lax.fori_loop(0, count, one, 0)


def greet(groups):
    barrier = pltpu.get_barrier_semaphore()
    for axis, count in groups:
        me = lax.axis_index(axis)

        def one(step, carry, axis=axis, count=count, me=me):
            pl.semaphore_signal(
                barrier,
                inc=1,
                device_id={axis: lax.rem(me + step, count)},
                device_id_type=MESH,
            )
            return carry

        lax.fori_loop(1, count, one, 0)


def await_greetings(groups):
    pl.semaphore_wait(pltpu.get_barrier_semaphore(), sum(count - 1 for _, count in groups))


def send_all(axis, count, pick, landing, sems):
    me = lax.axis_index(axis)

    def one(step, carry):
        peer = lax.rem(me + step, count)
        pltpu.make_async_remote_copy(
            src_ref=pick(peer),
            dst_ref=landing.at[me],
            send_sem=sems.at[0],
            recv_sem=sems.at[1],
            device_id={axis: peer},
            device_id_type=MESH,
        ).start()
        return carry

    lax.fori_loop(1, count, one, 0)


def wait_all(count, landing, sems):
    whole = landing.at[pl.ds(0, count - 1)]
    pltpu.make_async_copy(whole, whole, sems.at[1]).wait()
    pltpu.make_async_copy(whole, whole, sems.at[0]).wait()


def sum_slots(count, landing, wide=None):
    total = landing[0, :, 0:wide]
    for slot in range(1, count):
        total = total + landing[slot, :, 0:wide]
    return total


def stacked_dot(rows, matrix, dot):
    first, rest = high_and_rest(rows)
    second, third = high_and_rest(rest)
    stack = jnp.concatenate([first, second, third, jnp.zeros_like(rows)], axis=0).astype(BF16)
    full = dot(stack, matrix)
    return full[0:4] + full[4:8] + full[8:12]


def eliminate(work, first, last):
    size = work.shape[0]
    steps = size // 8
    row_at = lax.broadcasted_iota(I32, (8, 1), 0)

    def rows(step):
        return pl.ds(pl.multiple_of(step * 8, 8), 8)

    def reduce(panel):
        columns = [jnp.broadcast_to(panel[:, j : j + 1], (8, size)) for j in range(8)]
        left, right = panel[:, 0:size], panel[:, size:]
        for k in range(8):
            column = columns[k]
            inverse = 1.0 / column[k : k + 1, :]

            def clear(values, k=k, column=column, inverse=inverse):
                row = values[k : k + 1, :] * inverse
                return jnp.where(row_at == k, row, values - column * row)

            for j in range(k + 1, 8):
                columns[j] = clear(columns[j])
            left, right = clear(left), clear(right)
        return jnp.concatenate([left, right], axis=1)

    def less(values, panel):
        out = values
        for k in range(8):
            out = out - values[:, k : k + 1] * panel[k : k + 1, :]
        return out

    def rolled(values):
        return jnp.concatenate([pltpu.roll(values[:, 0:size], size - 8, 1), values[:, size:]], axis=1)

    def block(step, panel):
        following = rows(jnp.minimum(step + 1, steps - 1))
        upcoming = reduce(rolled(less(work[following, :], panel)))
        work[...] = rolled(less(work[...], panel))
        work[rows(step), :] = rolled(panel)
        return upcoming

    lax.fori_loop(first, last, block, reduce(work[rows(first), :]))


def body(
    n_sub, n_coarse,
    operator_there, coupling, coarse_rows, loads, lists, maps,
    solution, residual,
    operator, hot, spread, pick, inverse, near, direction, rounded, product, image, pieces,
    face_out, face_in, invd, scaled, gram, blend, picked, terms_mine,
    terms, terms_in, part_rows, part_in, solved_rows, solved_in, picks, picks_in,
    sums, sums_in, mid_rows, rows_in, mid_in, sums_out, maps_in, solver, inverter, sems, face_sems, load_sem,
):
    me, group = lax.axis_index("sub"), lax.axis_index("coarse")
    height, width = loads.shape
    corners = coupling.shape[0]
    slots = hot.shape[1]
    span = slots // 4
    row_length = n_sub // 4
    tiles = n_sub // 4
    column, row = lax.rem(me, row_length), me // row_length
    sides = (
        (-1, column > 0),
        (1, column < row_length - 1),
        (-row_length, row > 0),
        (row_length, row < 3),
    )

    def faces_start(rows):
        for face, (shift, there) in enumerate(sides):
            other = face ^ 1

            @pl.when(there)
            def _(face=face, shift=shift, other=other):
                pltpu.make_async_remote_copy(
                    src_ref=face_out.at[pl.ds(0, rows), pl.ds(face * span, span)],
                    dst_ref=face_in.at[pl.ds(0, rows), pl.ds(other * span, span)],
                    send_sem=face_sems.at[0, face],
                    recv_sem=face_sems.at[1, other],
                    device_id={"sub": me + shift},
                    device_id_type=MESH,
                ).start()

    def faces_wait(rows):
        for face, (_, there) in enumerate(sides):

            @pl.when(there)
            def _(face=face):
                view = face_in.at[pl.ds(0, rows), pl.ds(face * span, span)]
                pltpu.make_async_copy(view, view, face_sems.at[1, face]).wait()
                pltpu.make_async_copy(view, view, face_sems.at[0, face]).wait()

    def gather(rows):
        def one(step):
            at = lanes(step, TILE)
            full = nn(pieces[0 : 2 * rows, :], hot[:, at])
            face_out[0:rows, at] = full[0:rows] + full[rows : 2 * rows]

        loop(slots // TILE, one)

    def scatter_rows(rows, store):
        first, rest = high_and_rest(face_in[0:rows, :])
        pieces[0:rows, 0:slots] = first.astype(BF16)
        pieces[rows : 2 * rows, 0:slots] = rest.astype(BF16)

        def one(step):
            at = lanes(step, TILE)
            full = nt(pieces[0 : 2 * rows, 0:slots], hot[at, :])
            store(at, full[0:rows] + full[rows : 2 * rows])

        loop(width // TILE, one)

    per = height // row_length

    def part_of(index):
        return pl.ds(pl.multiple_of(index * per, per), per)

    def sum_parts(count, landing, wide):
        total = landing[0:per, 0:wide]
        for slot in range(1, count):
            total = total + landing[slot * per : (slot + 1) * per, 0:wide]
        return total

    def send_group(count, own, device, source, landing, sem, wide):
        def one(step, carry):
            peer = lax.rem(own + step, count)
            pltpu.make_async_remote_copy(
                src_ref=source(peer),
                dst_ref=landing.at[part_of(own), pl.ds(0, wide)],
                send_sem=sem.at[0],
                recv_sem=sem.at[1],
                device_id=device(peer),
                device_id_type=MESH,
            ).start()
            return carry

        lax.fori_loop(1, count, one, 0)

    def wait_group(count, landing, sem, wide):
        whole = landing.at[pl.ds(0, (count - 1) * per), pl.ds(0, wide)]
        pltpu.make_async_copy(whole, whole, sem.at[1]).wait()
        pltpu.make_async_copy(whole, whole, sem.at[0]).wait()

    def in_row(peer):
        return {"sub": row * row_length + peer}

    def in_column(peer):
        return {"sub": peer * row_length + column}

    def in_groups(peer):
        return {"coarse": peer}

    def all_sum_start(wide):
        sums_in[part_of(column), 0:wide] = sums[part_of(column), 0:wide]
        source = lambda peer: sums.at[part_of(peer), pl.ds(0, wide)]
        send_group(row_length, column, in_row, source, sums_in, sems.at[4], wide)

    def all_sum_stage(stage, count, own, device, landing, sem, total, wide):
        mid_rows[stage, :, 0:wide] = total
        landing[part_of(own), 0:wide] = total
        source = lambda peer: mid_rows.at[stage, :, pl.ds(0, wide)]
        send_group(count, own, device, source, landing, sem, wide)

    def all_sum_rows(wide):
        wait_group(row_length, sums_in, sems.at[4], wide)
        total = sum_parts(row_length, sums_in, wide)
        all_sum_stage(0, 4, row, in_column, rows_in, sems.at[8], total, wide)

    def all_sum_groups(wide):
        wait_group(4, rows_in, sems.at[8], wide)
        total = sum_parts(4, rows_in, wide)
        all_sum_stage(1, n_coarse, group, in_groups, mid_in, sems.at[5], total, wide)

    def all_sum_back(wide):
        wait_group(n_coarse, mid_in, sems.at[5], wide)
        total = sum_parts(n_coarse, mid_in, wide)
        all_sum_stage(2, row_length, column, in_row, sums_out, sems.at[6], total, wide)

    def all_sum_end(wide):
        wait_group(row_length, sums_out, sems.at[6], wide)

    def all_sum_finish(wide):
        all_sum_rows(wide)
        all_sum_groups(wide)
        all_sum_back(wide)
        all_sum_end(wide)

    face_in[...] = jnp.zeros_like(face_in)
    greet((("sub", n_sub), ("coarse", n_coarse)))
    load = pltpu.make_async_copy(operator_there, operator, load_sem)
    load.start()
    maps_in[me] = maps[...]

    def build_hot(step):
        at = lanes(step, LANES)
        index = lax.broadcasted_iota(I32, (width, LANES), 0)
        hot[:, at] = jnp.where(index == lists[:, at], 1.0, 0.0).astype(BF16)

    loop(slots // LANES, build_hot)
    eye = lax.broadcasted_iota(I32, (LANES, LANES), 0) == lax.broadcasted_iota(
        I32, (LANES, LANES), 1
    )
    face_rows = height + 8 + corners
    image[...] = jnp.zeros_like(image)
    rows_of = coarse_rows.shape[0]
    first, rest = high_and_rest(coarse_rows[...])
    inverse[...] = jnp.zeros_like(inverse)
    inverse[0:rows_of, :] = first.astype(BF16)
    inverse[256 : 256 + rows_of, :] = rest.astype(BF16)
    load.wait()
    for at in range(0, width, LANES):
        block = operator[at : at + LANES, at : at + LANES].astype(F32)
        image[0:1, at : at + LANES] = jnp.sum(jnp.where(eye, block, 0.0), axis=0, keepdims=True)
    values = jnp.concatenate([loads[...], image[0:8, :], coupling[...]], axis=0)
    first, rest = high_and_rest(values)
    pieces[0:face_rows, :] = first.astype(BF16)
    pieces[face_rows : 2 * face_rows, :] = rest.astype(BF16)
    gather(face_rows)
    await_greetings((("sub", n_sub), ("coarse", n_coarse)))
    faces_start(face_rows)
    send_all("sub", n_sub, lambda peer: maps, maps_in, sems.at[7])
    wait_all(n_sub, maps_in, sems.at[7])
    for t in range(tiles):
        both = sum_slots(4, maps_in.at[pl.ds(4 * t, 4)])
        at = slice(LANES * t, LANES * (t + 1))
        index = lax.broadcasted_iota(I32, (spread.shape[0], LANES), 0) + 1
        spread[:, at] = jnp.where(index == both[0:1, :], 1.0, 0.0).astype(BF16)
        index = lax.broadcasted_iota(I32, (pick.shape[0], LANES), 0) + 1
        pick[:, at] = jnp.where(index == both[1:2, :], 1.0, 0.0).astype(BF16)
    ones = jnp.ones((16, slots), BF16)

    def build_weight(step):
        at = lanes(step, TILE)
        scaled[:, at] = 1.0 / (1.0 + nt(ones, hot[at, :])[0:1])

    loop(width // TILE, build_weight)
    faces_wait(face_rows)

    product[...] = jnp.zeros_like(product)
    for face in range(4):
        at = slice(face * span, (face + 1) * span)
        product[corners * (face + 1) : corners * (face + 2), at] = face_in[height + 8 : face_rows, at]
    rounded[...] = product[...].astype(BF16)

    def build_near(step):
        at = lanes(step, TILE)
        tile = nt(rounded[:, 0:slots], hot[at, :])
        both = jnp.concatenate([coupling[:, at], tile[corners:]], axis=0)
        near[:, at] = both.astype(BF16)

    loop(width // TILE, build_near)

    rows = height + 16

    def finish_setup(at, added):
        combined = loads[:, at] + added[0:height]
        diagonal = image[0:1, at] + added[height : height + 1]
        residual[:, at] = combined
        invd[:, at] = 1.0 / diagonal
        direction[:, at] = combined / diagonal
        rounded[:, at] = direction[:, at].astype(BF16)
        solution[:, at] = jnp.zeros_like(combined)

    scatter_rows(rows, finish_setup)
    scaled[...] = scaled[...] * invd[...]
    start = nt(residual[...] * scaled[...], residual[...], HIGHEST)
    for p in range(n_sub):
        part = slice(4 * p, 4 * p + 4)
        sums[part, 0:LANES] = start[part, :]
    all_sum_start(LANES)

    lane_at = lax.broadcasted_iota(I32, (8, LANES), 1)
    own_lanes = lax.broadcasted_iota(I32, (height, LANES), 1) < corners
    slot_of = lax.rem(me, 4)

    def iteration(turn):
        mine = jnp.where(own_lanes, nt(rounded[...], near[...]), 0.0)
        terms_mine[...] = mine
        placed = mine
        for q in range(1, 4):
            placed = jnp.where(slot_of == q, pltpu.roll(mine, 32 * q, 1), placed)
        for p in range(n_sub):
            terms[p] = placed[4 * p : 4 * p + 4, :]
        terms_in[me] = terms[me]
        send_all("sub", n_sub, lambda peer: terms.at[peer], terms_in, sems.at[0])

        def multiply(step):
            at = lanes(step, TILE)
            tile = nn(rounded[...], operator[:, at])
            product[:, at] = tile
            first, rest = high_and_rest(tile)
            pieces[0:height, at] = first.astype(BF16)
            pieces[height : 2 * height, at] = rest.astype(BF16)

        loop(width // TILE, multiply)

        @pl.when(turn == 0)
        def _():
            all_sum_rows(LANES)

        wait_all(n_sub, terms_in, sems.at[0])
        row_tiles = [sum_slots(4, terms_in.at[pl.ds(4 * t, 4)]) for t in range(tiles)]
        partial = stacked_dot(jnp.concatenate(row_tiles, axis=1), spread[...], nt)
        part_rows[...] = partial
        part_in[group] = partial
        send_all("coarse", n_coarse, lambda peer: part_rows, part_in, sems.at[1])
        gather(height)
        faces_start(height)

        @pl.when(turn == 0)
        def _():
            all_sum_groups(LANES)

        wait_all(n_coarse, part_in, sems.at[1])

        @pl.when(turn == 0)
        def _():
            all_sum_back(LANES)

        wide = stacked_dot(sum_slots(n_coarse, part_in), inverse[...], nt)
        solved = wide[:, 0:256] + wide[:, 256:512]
        solved_rows[...] = solved
        solved_in[group] = solved
        send_all("coarse", n_coarse, lambda peer: solved_rows, solved_in, sems.at[2])
        both = nt(rounded[...], pieces[0 : 2 * height, :])
        curvature = both[:, 0:height] + both[:, height : 2 * height]

        def begin_inverse():
            inverter[:, 0:height] = gram[...]
            inverter[:, height:] = jnp.where(eye, 1.0, 0.0)

        @pl.when(turn > 0)
        def _():
            begin_inverse()
            eliminate(inverter, 0, 4)

        wait_all(n_coarse, solved_in, sems.at[2])
        everything = jnp.concatenate([solved_in[c] for c in range(n_coarse)], axis=1)
        chosen = stacked_dot(everything, pick[...], nn)
        doubled = jnp.concatenate([chosen, chosen], axis=0)
        for peer in range(n_sub):
            at_row, at_column = divmod(peer, row_length)
            sources = [(peer, 0)]
            if at_column > 0:
                sources.append((peer - 1, 1))
            if at_column < row_length - 1:
                sources.append((peer + 1, 2))
            if at_row > 0:
                sources.append((peer - row_length, 3))
            if at_row < 3:
                sources.append((peer + row_length, 4))
            total = jnp.zeros((8, LANES), F32)
            for source, place in sources:
                t = source // 4
                tile = doubled[:, LANES * t : LANES * (t + 1)]
                shift = (corners * place - 32 * (source % 4)) % LANES
                if shift:
                    tile = pltpu.roll(tile, shift, 1)
                here = (lane_at >= corners * place) & (lane_at < corners * (place + 1))
                total = jnp.where(here, tile, total)
            picks[peer] = total[0:4]
        picks_in[me] = picks[me]
        send_all("sub", n_sub, lambda peer: picks.at[peer], picks_in, sems.at[3])
        faces_wait(height)

        def add_faces(at, added):
            image[:, at] = product[:, at] + added

        scatter_rows(height, add_faces)

        @pl.when(turn > 0)
        def _():
            eliminate(inverter, 4, 8)

        @pl.when(turn == 0)
        def _():
            all_sum_end(LANES)
            gram[...] = sums_out[:, 0:LANES]
            begin_inverse()
            eliminate(inverter, 0, 4)

        wait_all(n_sub, picks_in, sems.at[3])
        for p in range(n_sub):
            picked[4 * p : 4 * p + 4, :] = picks_in[p]
        curvature = curvature + nt(
            terms_mine[...], jnp.where(own_lanes, picked[...], 0.0), HIGH
        )
        first, rest = high_and_rest(picked[...])
        stack = jnp.concatenate([first, rest], axis=0).astype(BF16)

        def add_corners(step):
            at = lanes(step, TILE)
            full = nn(stack, near[:, at])
            image[:, at] = image[:, at] + full[0:height] + full[height : 2 * height]

        loop(width // TILE, add_corners)
        for p in range(n_sub):
            part = slice(4 * p, 4 * p + 4)
            sums[part, 0:LANES] = curvature[part, :]

        @pl.when(turn < ITERS - 1)
        def _():
            weighted = image[...] * scaled[...]
            mixed = nt(weighted, residual[...], HIGH)
            square = nt(weighted, image[...], HIGH)
            for p in range(n_sub):
                part = slice(4 * p, 4 * p + 4)
                sums[part, LANES : 2 * LANES] = mixed[part, :]
                sums[part, 2 * LANES :] = square[part, :]
            all_sum_start(3 * LANES)
            eliminate(inverter, jnp.where(turn == 0, 4, 8), 16)
            all_sum_finish(3 * LANES)

        @pl.when(turn == ITERS - 1)
        def _():
            all_sum_start(LANES)
            all_sum_finish(LANES)

        solver[:, 0:LANES] = sums_out[:, 0:LANES]
        solver[:, height:] = gram[...]
        eliminate(solver, 0, height // 8)
        step_size = solver[:, height:]
        step_turned = step_size.T

        @pl.when(turn < ITERS - 1)
        def _():
            cross = nn(step_turned, sums_out[:, LANES : 2 * LANES], HIGHEST)
            twice = nn(step_turned, nn(sums_out[:, 2 * LANES :], step_size, HIGHEST), HIGHEST)
            fresh = gram[...] - cross - cross.T + twice
            blend[...] = nn(fresh, inverter[:, height:], HIGHEST)
            gram[...] = fresh

        factors = jnp.concatenate([step_turned, blend[...]], axis=0)

        def update(step):
            at = lanes(step, TILE)
            moved = nn(factors, direction[:, at], HIGH)
            solution[:, at] = solution[:, at] + moved[0:height]
            left = residual[:, at] - nn(step_turned, image[:, at], HIGH)
            residual[:, at] = left
            ahead = left * invd[:, at] + moved[height : 2 * height]
            direction[:, at] = ahead
            rounded[:, at] = ahead.astype(BF16)

        loop(width // TILE, update)

    blend[...] = jnp.zeros_like(blend)
    loop(ITERS, iteration)


def hand_on(solved, left, solved_out, left_out):
    solved_out[...] = solved[...]
    left_out[...] = left[...]


def local(
    local_operators, couplings, coarse_inverse, local_loads, face_lists, face_counts, corner_map
):
    slot_lists = face_lists[0]
    face_total, slot_total = slot_lists.shape
    _, height, width = local_loads.shape
    corners = couplings.shape[1]
    n_sub, n_coarse = lax.axis_size("sub"), lax.axis_size("coarse")
    slots = face_total * slot_total
    rows, coarse_total = coarse_inverse.shape
    face_rows = height + 8 + corners
    split = n_sub // 4 * LANES

    usable = lax.broadcasted_iota(I32, (face_total, slot_total), 1) < face_counts[0][:, None]
    marked = jnp.where(usable, slot_lists, -1).reshape(1, slots)
    place = corner_map // rows * 256 + corner_map % rows
    both = jnp.concatenate([corner_map, place], axis=0) + 1
    maps = lax.dynamic_update_slice(
        jnp.zeros((2, LANES), I32), both, (0, lax.rem(lax.axis_index("sub"), 4) * 32)
    )
    result = [jax.ShapeDtypeStruct((height, width), F32)] * 2
    per = height // n_sub
    scratch = [
        pltpu.VMEM((width, width), BF16),
        pltpu.VMEM((width, slots), BF16),
        pltpu.VMEM((coarse_total, split), BF16),
        pltpu.VMEM((n_coarse * 256, split), BF16),
        pltpu.VMEM((512, coarse_total), BF16),
        pltpu.VMEM((LANES, width), BF16),
        pltpu.VMEM((height, width), F32),
        pltpu.VMEM((height, width), BF16),
        pltpu.VMEM((height, width), F32),
        pltpu.VMEM((height, width), F32),
        pltpu.VMEM((2 * face_rows, width), BF16),
        pltpu.VMEM((face_rows, slots), F32),
        pltpu.VMEM((face_rows, slots), F32),
        pltpu.VMEM((1, width), F32),
        pltpu.VMEM((1, width), F32),
        pltpu.VMEM((height, height), F32),
        pltpu.VMEM((height, height), F32),
        pltpu.VMEM((height, LANES), F32),
        pltpu.VMEM((height, LANES), F32),
        pltpu.VMEM((n_sub, per, LANES), F32),
        pltpu.VMEM((n_sub, per, LANES), F32),
        pltpu.VMEM((per, coarse_total), F32),
        pltpu.VMEM((n_coarse, per, coarse_total), F32),
        pltpu.VMEM((per, 256), F32),
        pltpu.VMEM((n_coarse, per, 256), F32),
        pltpu.VMEM((n_sub, per, LANES), F32),
        pltpu.VMEM((n_sub, per, LANES), F32),
        pltpu.VMEM((8 * (height // 8), 3 * height), F32),
        pltpu.VMEM((8 * (height // 8), 3 * height), F32),
        pltpu.VMEM((3, height // 8, 3 * height), F32),
        pltpu.VMEM((4 * (height // 8), 3 * height), F32),
        pltpu.VMEM((n_coarse * (height // 8), 3 * height), F32),
        pltpu.VMEM((8 * (height // 8), 3 * height), F32),
        pltpu.VMEM((n_sub, 2, LANES), I32),
        pltpu.VMEM((height, 2 * height), F32),
        pltpu.VMEM((height, 2 * height), F32),
        pltpu.SemaphoreType.DMA((9, 2)),
        pltpu.SemaphoreType.DMA((2, 4)),
        pltpu.SemaphoreType.DMA,
    ]
    solved, left = pl.pallas_call(
        lambda *refs: body(n_sub, n_coarse, *refs),
        out_shape=result,
        in_specs=[pl.BlockSpec(memory_space=pl.ANY)] + [VMEM] * 5,
        out_specs=[VMEM] * 2,
        scratch_shapes=scratch,
        compiler_params=pltpu.CompilerParams(
            collective_id=0, has_side_effects=True, vmem_limit_bytes=60 << 20
        ),
    )(local_operators[0], couplings[0].astype(F32), coarse_inverse, local_loads[0], marked, maps)
    solved, left = pl.pallas_call(
        hand_on, out_shape=result, in_specs=[VMEM] * 2, out_specs=[VMEM] * 2
    )(solved, left)
    return (solved[None], left[None])


def solution(mesh):
    return jax.shard_map(
        local,
        mesh=mesh,
        in_specs=(
            P(("coarse", "sub"), None, None),
            P(("coarse", "sub"), None, None),
            P("coarse", None),
            P(("coarse", "sub"), None, None),
            P(("coarse", "sub"), None, None),
            P(("coarse", "sub"), None),
            P(("coarse", "sub"), None),
        ),
        out_specs=(P(("coarse", "sub"), None, None), P(("coarse", "sub"), None, None)),
        check_vma=False,
    )
```
